512 devices in a mesh: ens: 4 (over x), grid: 128 (over y, z, core).
Axes of the slice: x: 4, y: 8, z: 8, core: 2. Of those that a mesh axis runs over, the one named last changes fastest.
Arguments:
- grid_latent: bfloat16 [4, 131072, 512], P('ens', 'grid'), may hold values from -6 to 6
- mesh_latent: bfloat16 [4, 16384, 512], P('ens', 'grid'), may hold values from -6 to 6
- cotangent: bfloat16 [4, 16384, 512], P('ens', 'grid'), may hold values from -6 to 6
- edge_weights: bfloat16 [1024, 2, 128, 128], P('grid'), may hold values from -0.125 to 0.125
- edge_targets: int32 [1024, 2], P('grid'), may hold values from 0 to 127, as said below
- mesh_weights: bfloat16 [128, 2, 128, 128], P('grid'), may hold values from -0.375 to 0.375
- mesh_sources: int32 [128, 2], P('grid'), may hold values from 0 to 127, as said below
- encode_weight: bfloat16 [512, 512], replicated, may hold values from -0.25 to 0.25
- aggregate_weight: bfloat16 [512, 512], replicated, may hold values from -0.25 to 0.25
- process_weight: bfloat16 [512, 512], replicated, may hold values from -0.25 to 0.25
Outputs:
- result: bfloat16 [4, 16384, 512], P('ens', 'grid')
- grid_grad: bfloat16 [4, 131072, 512], P('ens', 'grid')
- grad_encode: float32 [512, 512], P('grid')
The draws below stay inside these ranges and needn't reach their ends.
Inputs may be any that keep to these rules, and one draw needn't show every extreme that they name: `edge_targets`: row b names 2 different mesh blocks, each at most one away from b // 8. `mesh_sources`: row t names 2 different mesh blocks, each at most one away from t.
All inputs are finite; a program needn't handle non-finite values.
Results may differ from the reference program's by a relative error of at most 0.018.
Values may be sent and summed in bfloat16 or wider, within the bound.
No kernel may reach another device: no remote copies, remote signals or barrier semaphores. Data moves between devices by JAX's collectives and lax.ppermute only.
A program may use at most 64 MiB of HBM per device.

```python
import jax
import jax.numpy as jnp
from jax import lax

D = 512
BLK = 128
K = 2
KM = 2
GB_DEV = 8
MEMBERS = 4
GRID_BLOCKS = 1024
GRID = 131072
MESH_BLOCKS = 128
MESH = 16384


def pick_near(key, count, spread, picks):
    owner = jnp.arange(count, dtype=jnp.int32) // spread
    offsets = jnp.arange(3, dtype=jnp.int32)
    scores = jax.random.randint(key, (count, 3), 0, 1000, dtype=jnp.int32) * 3 + offsets
    nearby = owner[:, None] + offsets - 1
    inside = (nearby >= 0) & (nearby < MESH_BLOCKS)
    scores = jnp.where(inside, scores, -1)
    unused, order = lax.top_k(scores, picks)
    return jnp.take_along_axis(nearby, order, 1).astype(jnp.int32)


def draw_edge_targets(key, part):
    key = jax.random.fold_in(key, 11)
    return pick_near(key, GRID_BLOCKS, GB_DEV, K)


def draw_mesh_sources(key, part):
    key = jax.random.fold_in(key, 17)
    return pick_near(key, MESH_BLOCKS, 1, KM)


def block_levels(stream_key, extent, split, low, largest):
    loudness = 1.0
    for dim, blocks in split:
        steps = jax.random.uniform(jax.random.fold_in(jax.random.fold_in(stream_key, 6), dim), (blocks,), jnp.float32, low / len(split), largest / len(split))
        loudness = loudness * jnp.repeat(jnp.exp(steps), extent[dim] // blocks).reshape((-1,) + (1,) * (len(extent) - 1 - dim))
    return loudness


def bell_draw(rng, extent, deviation, bound, cuts=(), kind=jnp.bfloat16):
    values = jax.random.normal(rng, extent, jnp.float32) * deviation
    if len(cuts) > 0:
        values = block_levels(rng, extent, cuts, -0.22, 0.18) * values
    return jnp.clip(values, min=-bound, max=bound).astype(kind)


def setup_inputs(seed: int = 0) -> dict:
    splits = jax.random.split(jax.random.key(seed), 11)
    grid_latent = bell_draw(splits[0], (MEMBERS, GRID, D), 1.0, 6.0, ((0, 4), (1, 128)))
    mesh_latent = bell_draw(splits[1], (MEMBERS, MESH, D), 1.0, 6.0, ((0, 4), (1, 128)))
    cotangent = bell_draw(splits[2], (MEMBERS, MESH, D), 1.0, 6.0, ((0, 4), (1, 128)))
    edge_weights = bell_draw(splits[3], (GRID_BLOCKS, K, BLK, BLK), (GB_DEV * K * BLK) ** -0.5, 0.125, ((0, 128),))
    edge_targets = draw_edge_targets(jax.random.fold_in(splits[10], 71), 0)
    mesh_weights = bell_draw(splits[5], (MESH_BLOCKS, KM, BLK, BLK), (KM * BLK) ** -0.5, 0.375, ((0, 128),))
    mesh_sources = draw_mesh_sources(jax.random.fold_in(splits[10], 71), 0)
    encode_weight = bell_draw(splits[7], (D, D), D ** -0.5, 0.25)
    aggregate_weight = bell_draw(splits[8], (D, D), D ** -0.5, 0.25)
    process_weight = bell_draw(splits[9], (D, D), D ** -0.5, 0.25)
    return dict(grid_latent=grid_latent, mesh_latent=mesh_latent, cotangent=cotangent, edge_weights=edge_weights, edge_targets=edge_targets, mesh_weights=mesh_weights, mesh_sources=mesh_sources, encode_weight=encode_weight, aggregate_weight=aggregate_weight, process_weight=process_weight)


def silu_slope(value):
    sig = jax.nn.sigmoid(value)
    return sig * (1.0 + value * (1.0 - sig))


def spread_blocks(parts):
    zero_block = jnp.zeros_like(parts[:1, 0])
    from_lower = jnp.concatenate([zero_block, parts[:-1, 2]], 0)
    from_upper = jnp.concatenate([parts[1:, 0], zero_block], 0)
    return parts[:, 1] + from_lower + from_upper


def reference(grid_latent, mesh_latent, cotangent, edge_weights, edge_targets, mesh_weights, mesh_sources, encode_weight, aggregate_weight, process_weight):
    owner = jnp.arange(GRID_BLOCKS, dtype=jnp.int32) // GB_DEV
    three = jnp.arange(3, dtype=jnp.int32)
    target_pick = ((edge_targets - owner[:, None] + 1)[:, :, None] == three).astype(jnp.float32)
    ident = jnp.arange(MESH_BLOCKS, dtype=jnp.int32)
    source_pick = ((mesh_sources - ident[:, None] + 1)[:, :, None] == three).astype(jnp.float32)
    edge_float = edge_weights.astype(jnp.float32)
    mesh_float = mesh_weights.astype(jnp.float32)

    def member(packed):
        grid_x, mesh_h, upstream_in = packed
        encoded = jnp.dot(grid_x, encode_weight, preferred_element_type=jnp.float32)
        messages = jax.nn.silu(encoded).astype(jnp.bfloat16).reshape(GRID_BLOCKS, BLK, D)
        products = jnp.einsum('bkac,bcd->bkad', edge_float, messages.astype(jnp.float32))
        panels = jnp.einsum('bkj,bkad->bjad', target_pick, products)
        panels = panels.reshape(MESH_BLOCKS, GB_DEV, 3, BLK, D).sum(1).astype(jnp.bfloat16)
        aggregated = spread_blocks(panels.astype(jnp.float32)).astype(jnp.bfloat16).reshape(MESH, D)
        mesh_pre = jnp.dot(aggregated, aggregate_weight, preferred_element_type=jnp.float32)
        updated = (mesh_h.astype(jnp.float32) + jax.nn.silu(mesh_pre)).astype(jnp.bfloat16)
        zero_block = jnp.zeros((1, BLK, D), jnp.bfloat16)
        padded = jnp.concatenate([zero_block, updated.reshape(MESH_BLOCKS, BLK, D), zero_block], 0)
        chosen = padded[(mesh_sources + 1).astype(jnp.int32)]
        processed = jnp.einsum('tkab,tkbd->tad', mesh_float, chosen.astype(jnp.float32))
        processed = processed.astype(jnp.bfloat16).reshape(MESH, D)
        proc_pre = jnp.dot(processed, process_weight, preferred_element_type=jnp.float32)
        result = (updated.astype(jnp.float32) + jax.nn.silu(proc_pre)).astype(jnp.bfloat16)
        upstream = upstream_in.astype(jnp.float32)
        proc_delta = (upstream * silu_slope(proc_pre)).astype(jnp.bfloat16)
        proc_back = jnp.dot(proc_delta, process_weight.T, preferred_element_type=jnp.float32)
        proc_back = proc_back.astype(jnp.bfloat16).reshape(MESH_BLOCKS, BLK, D)
        back = jnp.einsum('tkab,tad->tkbd', mesh_float, proc_back.astype(jnp.float32))
        pushed = jnp.einsum('tkj,tkbd->tjbd', source_pick, back).astype(jnp.bfloat16)
        mesh_grad = upstream + spread_blocks(pushed.astype(jnp.float32)).reshape(MESH, D)
        mesh_delta = (mesh_grad * silu_slope(mesh_pre)).astype(jnp.bfloat16)
        agg_grad = jnp.dot(mesh_delta, aggregate_weight.T, preferred_element_type=jnp.float32)
        agg_grad = agg_grad.astype(jnp.bfloat16).reshape(MESH_BLOCKS, BLK, D)
        padded_grad = jnp.concatenate([zero_block, agg_grad, zero_block], 0)
        picked = padded_grad[(edge_targets + 1).astype(jnp.int32)]
        message_grad = jnp.einsum('bkac,bkad->bcd', edge_float, picked.astype(jnp.float32)).reshape(GRID, D)
        enc_delta = (message_grad * silu_slope(encoded)).astype(jnp.bfloat16)
        grad_enc = jnp.dot(grid_x.T, enc_delta, preferred_element_type=jnp.float32)
        grid_grad = jnp.dot(enc_delta, encode_weight.T, preferred_element_type=jnp.float32).astype(jnp.bfloat16)
        return result, grid_grad, grad_enc

    result, grid_grad, grad_enc = lax.map(member, (grid_latent, mesh_latent, cotangent))
    grid_scale = 1.0 / (float(MEMBERS * GRID) ** 0.5)
    grad_encode = jnp.sum(grad_enc, 0) * grid_scale
    return (result, grid_grad, grad_encode)
```

```python
import jax
import jax.numpy as jnp
from jax import lax
from jax.sharding import Mesh
from jax.sharding import PartitionSpec as P

BF = jnp.bfloat16
F32 = jnp.float32
GRID = ("y", "z", "core")


def grid_split(count):
    cores = 2
    chips = count // cores
    ys = 1
    while ys * ys < chips:
        ys *= 2
    return ys, chips // ys, cores


def swap_pairs(count):
    mates = [(2 * c, 2 * c + 1) for c in range(count // 2)]
    across = [(2 * c + 1, 2 * c + 2) for c in range(count // 2 - 1)]
    both = lambda pairs: pairs + [(b, a) for a, b in pairs]
    return both(mates), both(across)


def dot(a, b, ca, cb):
    return lax.dot_general(a, b, (((ca,), (cb,)), ((), ())), preferred_element_type=F32)


def silu_slope(value):
    sig = jax.nn.sigmoid(value)
    return sig * (1.0 + value * (1.0 - sig))


def spread(weights, slots):
    blocks, picks, rows, cols = weights.shape
    three = jnp.arange(3, dtype=jnp.int32)
    hit = slots[:, :, None] == three
    laid = sum(
        jnp.where(hit[:, k, :, None, None], weights[:, k, None], jnp.zeros((), BF))
        for k in range(picks)
    )
    return laid.transpose(1, 2, 0, 3).reshape(3 * rows, blocks * cols)


def on_device(
    grid_latent, mesh_latent, cotangent, edge_weights, edge_targets,
    mesh_weights, mesh_sources, encode_weight, aggregate_weight, process_weight,
):
    members = lax.axis_size("ens")
    bands = lax.axis_size(GRID)
    here = lax.axis_index(GRID)
    core = lax.axis_index("core")
    sign = 1 - 2 * core
    mates, across = swap_pairs(bands)
    blocks, _, rows, _ = edge_weights.shape
    width = grid_latent.shape[2]
    half = width // 2

    def exchange(to_across, to_mate):
        from_across = lax.ppermute(to_across, GRID, across)
        from_mate = lax.ppermute(to_mate, GRID, mates)
        return from_across, from_mate

    edge_slots = (edge_targets - here) * sign + 1
    mesh_slots = (mesh_sources - here) * sign + 1
    edges = spread(edge_weights, edge_slots)
    grid_x = grid_latent[0]
    encoded = dot(grid_x, encode_weight, 1, 0)
    messages = jax.nn.silu(encoded).astype(BF)
    panels = dot(edges, messages, 1, 0).astype(BF)
    a, m = exchange(panels[:rows], panels[2 * rows :])
    aggregated = (
        panels[rows : 2 * rows].astype(F32) + a.astype(F32) + m.astype(F32)
    ).astype(BF)
    mesh_pre = dot(aggregated, aggregate_weight, 1, 0)
    updated = (mesh_latent[0].astype(F32) + jax.nn.silu(mesh_pre)).astype(BF)
    a, m = exchange(updated, updated)
    nearby = jnp.concatenate([a, updated, m], 0)
    mixing = spread(mesh_weights[0][None].transpose(0, 1, 3, 2), mesh_slots)
    processed = dot(mixing, nearby, 0, 0).astype(BF)
    proc_pre = dot(processed, process_weight, 1, 0)
    result = (updated.astype(F32) + jax.nn.silu(proc_pre)).astype(BF)
    upstream = cotangent[0].astype(F32)
    proc_delta = (upstream * silu_slope(proc_pre)).astype(BF)
    proc_back = dot(proc_delta, process_weight, 1, 1).astype(BF)
    pushed = dot(mixing, proc_back, 1, 0).astype(BF)
    a, m = exchange(pushed[:rows], pushed[2 * rows :])
    mesh_grad = upstream + pushed[rows : 2 * rows].astype(F32) + a.astype(F32) + m.astype(F32)
    mesh_delta = (mesh_grad * silu_slope(mesh_pre)).astype(BF)
    agg_grad = dot(mesh_delta, aggregate_weight, 1, 1).astype(BF)
    a, m = exchange(agg_grad, agg_grad)
    returned = jnp.concatenate([a, agg_grad, m], 0)
    message_grad = dot(edges, returned, 0, 0)
    enc_delta = (message_grad * silu_slope(encoded)).astype(BF)
    theirs = lax.dynamic_slice_in_dim(enc_delta, (1 - core) * half, half, 1)
    ours = lax.dynamic_slice_in_dim(enc_delta, core * half, half, 1)
    arrived = lax.ppermute(dot(grid_x, theirs, 0, 0).astype(BF), GRID, mates)
    grid_grad = dot(enc_delta, encode_weight, 1, 1).astype(BF)
    pair = (dot(grid_x, ours, 0, 0) + arrived.astype(F32)).astype(BF)
    chips = bands // 2
    share = width // chips
    parts = lax.all_to_all(pair.reshape(chips, share, half), ("y", "z"), 0, 0)
    column = parts.astype(F32).sum(0)
    scale = 1.0 / float(members * blocks * rows * bands) ** 0.5
    column = (column * scale).reshape(1, 2, share // 2, half)
    column = jnp.broadcast_to(column, (members,) + column.shape[1:])
    column = column.reshape(members * 2, share // 2, half)
    last = lax.all_to_all(column, ("ens", "core"), 0, 0)
    last = last.reshape(members, 2, share // 2, half).sum(0)
    final = last.transpose(1, 0, 2).reshape(share // 2, width)
    return result[None], grid_grad[None], final


def solution(mesh):
    ens, bands = mesh.devices.shape
    fine = Mesh(mesh.devices.reshape((ens,) + grid_split(bands)), ("ens",) + GRID)
    return jax.shard_map(
        on_device,
        mesh=fine,
        in_specs=(
            P("ens", GRID, None),
            P("ens", GRID, None),
            P("ens", GRID, None),
            P(GRID, None, None, None),
            P(GRID, None),
            P(GRID, None, None, None),
            P(GRID, None),
            P(),
            P(),
            P(),
        ),
        out_specs=(P("ens", GRID, None), P("ens", GRID, None), P(GRID, None)),
        check_vma=False,
    )
```

```python
import functools

import jax
import jax.numpy as jnp
from jax import lax
from jax.experimental import pallas as pl
from jax.experimental.pallas import tpu as pltpu
from jax.sharding import Mesh
from jax.sharding import PartitionSpec as P

BF = jnp.bfloat16
F32 = jnp.float32
GRID = ("y", "z", "core")


def grid_split(count):
    cores = 2
    chips = count // cores
    ys = 1
    while ys * ys < chips:
        ys *= 2
    return ys, chips // ys, cores


def swap_pairs(count):
    mates = [(2 * c, 2 * c + 1) for c in range(count // 2)]
    across = [(2 * c + 1, 2 * c + 2) for c in range(count // 2 - 1)]
    both = lambda pairs: pairs + [(b, a) for a, b in pairs]
    return both(mates), both(across)


def dot(a, b, ca, cb):
    return lax.dot_general(a, b, (((ca,), (cb,)), ((), ())), preferred_element_type=F32)


def sigmoid(value):
    return 0.5 * jnp.tanh(0.5 * value) + 0.5


def silu_and_slope(value):
    sig = sigmoid(value)
    lifted = value * sig
    return lifted, sig + lifted - lifted * sig


def call(kernel, outs, scratch, flops, moved, *operands, copied=False):
    floats = pltpu.HBM if copied else pltpu.VMEM
    specs = [
        pl.BlockSpec(memory_space=pltpu.SMEM if o.dtype == jnp.int32 else floats)
        for o in operands
    ]
    single = len(outs) == 1
    shapes = [jax.ShapeDtypeStruct(shape, kind) for shape, kind in outs]
    vmem = [pl.BlockSpec(memory_space=pltpu.VMEM) for _ in outs]
    return pl.pallas_call(
        kernel,
        out_shape=shapes[0] if single else shapes,
        in_specs=specs,
        out_specs=vmem[0] if single else vmem,
        scratch_shapes=[pltpu.VMEM(*o) if isinstance(o, tuple) else o for o in scratch],
        compiler_params=pltpu.CompilerParams(vmem_limit_bytes=(60 if copied else 24) << 20),
        cost_estimate=pl.CostEstimate(flops=flops, bytes_accessed=moved, transcendentals=0),
    )(*operands)


def slot_of(block):
    here = lax.axis_index(GRID)
    sign = 1 - 2 * lax.axis_index("core")
    return jnp.clip((block - here) * sign + 1, 0, 2)


def encode_kernel(
    targets, x_hbm, weight_hbm, edges_hbm, across, own, mate, slope, laid, x, weight, edges, messages, arrived
):
    blocks, picks, rows, cols = edges.shape
    nodes = x.shape[0]
    chunks = 4
    step = nodes // chunks
    pieces = [slice(i * step, (i + 1) * step) for i in range(chunks)]
    copies = [pltpu.make_async_copy(weight_hbm, weight, arrived.at[0])]
    for i in range(chunks):
        copies.append(pltpu.make_async_copy(x_hbm.at[pieces[i]], x.at[pieces[i]], arrived.at[1 + i]))
    copies.append(pltpu.make_async_copy(edges_hbm, edges, arrived.at[1 + chunks]))
    for copy in copies:
        copy.start()
    laid[...] = jnp.zeros_like(laid)
    copies[0].wait()
    for i in range(chunks):
        copies[1 + i].wait()
        lifted, slanted = silu_and_slope(dot(x[pieces[i], :], weight[...], 1, 0))
        slope[pieces[i], :] = slanted.astype(BF)
        messages[pieces[i], :] = lifted.astype(BF)
    copies[1 + chunks].wait()
    for b in range(blocks):
        for k in range(picks):
            at = pl.ds(pl.multiple_of(slot_of(targets[k, b]) * rows, rows), rows)
            laid[at, b * cols : (b + 1) * cols] = edges[b, k]
    across[...] = dot(laid[:rows, :], messages[...], 1, 0).astype(BF)
    mate[...] = dot(laid[2 * rows :, :], messages[...], 1, 0).astype(BF)
    own[...] = dot(laid[rows : 2 * rows, :], messages[...], 1, 0).astype(BF)


def turn_kernel(laid, turned):
    turned[...] = laid[...].T


def sort_kernel(share, x, sorted_x):
    width = x.shape[1]
    row = lax.broadcasted_iota(jnp.int32, (width, width), 0)
    col = lax.broadcasted_iota(jnp.int32, (width, width), 1)
    half = width // 2
    ours = row // half
    inner = row % half
    core = lax.axis_index("core")
    side = jnp.where(ours == 1, core, 1 - core)
    wanted = (inner // share) * (2 * share) + side * share + inner % share
    pick = jnp.where(col == wanted, 1.0, 0.0).astype(BF)
    sorted_x[...] = dot(pick, x[...], 1, 1).astype(BF)


def update_kernel(across, own, mate, latent, weight, updated, again, slope):
    arrived = own[...].astype(F32) + across[...].astype(F32) + mate[...].astype(F32)
    lifted, slanted = silu_and_slope(dot(arrived.astype(BF), weight[...], 1, 0))
    slope[...] = slanted
    fresh = (latent[...].astype(F32) + lifted).astype(BF)
    updated[...] = fresh
    again[...] = fresh


def mix_kernel(sources, mixing, laid, turned):
    rows = mixing.shape[1]
    laid[...] = jnp.zeros_like(laid)
    for k in range(mixing.shape[0]):
        at = pl.ds(pl.multiple_of(slot_of(sources[0, k]) * rows, rows), rows)
        laid[:, at] = mixing[k]
    turned[...] = laid[...].T


def process_kernel(
    across, own, mate, mixing, turned, weight, cotangent, result, to_across, to_own, to_mate, near
):
    rows = own.shape[0]
    near[:rows, :] = across[...]
    near[rows : 2 * rows, :] = own[...]
    near[2 * rows :, :] = mate[...]
    processed = dot(mixing[...], near[...], 1, 0).astype(BF)
    lifted, slanted = silu_and_slope(dot(processed, weight[...], 1, 0))
    result[...] = (own[...].astype(F32) + lifted).astype(BF)
    delta = (cotangent[...].astype(F32) * slanted).astype(BF)
    back = dot(delta, weight[...], 1, 1).astype(BF)
    pushed = dot(turned[...], back, 1, 0).astype(BF)
    to_across[...], to_own[...], to_mate[...] = pushed[:rows], pushed[rows : 2 * rows], pushed[2 * rows :]


def return_kernel(across, own, mate, cotangent, slope, weight, grad, again):
    total = cotangent[...].astype(F32) + own[...].astype(F32)
    total = total + across[...].astype(F32) + mate[...].astype(F32)
    fresh = dot((total * slope[...]).astype(BF), weight[...], 1, 1).astype(BF)
    grad[...] = fresh
    again[...] = fresh


def message_kernel(across, own, mate, turned, slope, sorted_x, delta, theirs, near):
    rows = own.shape[0]
    near[:rows, :] = across[...]
    near[rows : 2 * rows, :] = own[...]
    near[2 * rows :, :] = mate[...]
    nodes = slope.shape[0]
    step = nodes // 4
    for i in range(4):
        at = slice(i * step, (i + 1) * step)
        grad = dot(turned[at, :], near[...], 1, 0)
        delta[at, :] = (grad * slope[at, :].astype(F32)).astype(BF)
    theirs[...] = dot(sorted_x[: theirs.shape[0], :], delta[...], 1, 0).astype(BF)


def gradient_kernel(sorted_x, delta, weight, ours, grid_grad):
    ours[...] = dot(sorted_x[ours.shape[0] :, :], delta[...], 1, 0)
    step = delta.shape[0] // 4
    for i in range(4):
        at = slice(i * step, (i + 1) * step)
        grid_grad[at, :] = dot(delta[at, :], weight[...], 1, 1).astype(BF)


def on_device(
    grid_latent, mesh_latent, cotangent, edge_weights, edge_targets,
    mesh_weights, mesh_sources, encode_weight, aggregate_weight, process_weight,
):
    members = lax.axis_size("ens")
    bands = lax.axis_size(GRID)
    mates, across_pairs = swap_pairs(bands)
    blocks, _, rows, _ = edge_weights.shape
    width = grid_latent.shape[2]
    half = width // 2

    def exchange(to_across, to_mate):
        from_mate = lax.ppermute(to_mate, GRID, mates)
        from_across = lax.ppermute(to_across, GRID, across_pairs)
        return from_across, from_mate

    nodes = blocks * rows
    grid_x = grid_latent[0]
    block = ((rows, width), BF)
    near = ((3 * rows, width), BF)
    to_across, own, to_mate, slope, laid = call(
        encode_kernel,
        [block, block, block, ((nodes, width), BF), ((3 * rows, nodes), BF)],
        [
            (grid_x.shape, BF), (encode_weight.shape, BF), (edge_weights.shape, BF),
            ((nodes, width), BF), pltpu.SemaphoreType.DMA((6,)),
        ],
        2 * nodes * width * (width + 3 * rows), 4 << 20,
        edge_targets.T, grid_x, encode_weight, edge_weights,
        copied=True,
    )
    across, mate = exchange(to_across, to_mate)
    sources, _ = lax.optimization_barrier((mesh_sources, slope))
    mixing, mixing_turned = call(
        mix_kernel, [((rows, 3 * rows), BF), ((3 * rows, rows), BF)], [], 0, 1 << 18,
        sources, mesh_weights[0],
    )
    updated, again, mesh_slope = call(
        update_kernel, [block, block, ((rows, width), F32)], [],
        2 * rows * width * width, 1 << 20,
        across, own, mate, mesh_latent[0], aggregate_weight,
    )
    across, mate = exchange(again, updated)
    later, grid_y, _ = lax.optimization_barrier((laid, grid_x, updated))
    turned = call(turn_kernel, [((nodes, 3 * rows), BF)], [], 0, 2 << 20, later)
    result, to_across, own, to_mate = call(
        process_kernel, [block] * 4, [near],
        4 * rows * width * width, 1 << 20,
        across, updated, mate, mixing, mixing_turned, process_weight, cotangent[0],
    )
    across, mate = exchange(to_across, to_mate)
    share = width // bands
    grid_y, _ = lax.optimization_barrier((grid_y, own))
    sorted_x = call(
        functools.partial(sort_kernel, share), [((width, nodes), BF)], [],
        2 * nodes * width * width, 2 << 20,
        grid_y,
    )
    agg_grad, again = call(
        return_kernel, [block, block], [],
        2 * rows * width * width, 1 << 20,
        across, own, mate, cotangent[0], mesh_slope, aggregate_weight,
    )
    across, mate = exchange(again, agg_grad)
    enc_delta, theirs = call(
        message_kernel, [((nodes, width), BF), ((half, width), BF)], [near],
        2 * nodes * width * (3 * rows + half), 4 << 20,
        across, agg_grad, mate, turned, slope, sorted_x,
    )
    arrived = lax.ppermute(theirs, GRID, mates)
    ours, grid_grad = call(
        gradient_kernel, [((half, width), F32), ((nodes, width), BF)], [],
        2 * nodes * width * (width + half), 4 << 20,
        sorted_x, enc_delta, encode_weight,
    )
    pair = (ours + arrived.astype(F32)).astype(BF)
    chips = bands // 2
    parts = lax.all_to_all(pair.reshape(chips, share, width), ("y", "z"), 0, 0)
    scale = 1.0 / float(members * nodes * bands) ** 0.5
    summed = parts.astype(F32).sum(0) * scale
    summed = jnp.broadcast_to(summed, (members, share, width))
    final = lax.all_to_all(summed, "ens", 0, 0).sum(0)
    return result[None], grid_grad[None], final


def solution(mesh):
    ens, bands = mesh.devices.shape
    fine = Mesh(mesh.devices.reshape((ens,) + grid_split(bands)), ("ens",) + GRID)
    return jax.shard_map(
        on_device,
        mesh=fine,
        in_specs=(
            P("ens", GRID, None),
            P("ens", GRID, None),
            P("ens", GRID, None),
            P(GRID, None, None, None),
            P(GRID, None),
            P(GRID, None, None, None),
            P(GRID, None),
            P(),
            P(),
            P(),
        ),
        out_specs=(P("ens", GRID, None), P("ens", GRID, None), P(GRID, None)),
        check_vma=False,
    )
```

```python
import functools

import jax
import jax.numpy as jnp
from jax import lax
from jax.experimental import pallas as pl
from jax.experimental.pallas import tpu as pltpu
from jax.sharding import Mesh
from jax.sharding import PartitionSpec as P

BF = jnp.bfloat16
F32 = jnp.float32
ENCODE_VMEM = 55992320
GRID = ("y", "z", "core")


def grid_split(count):
    cores = 2
    chips = count // cores
    ys = 1
    while ys * ys < chips:
        ys *= 2
    return ys, chips // ys, cores


def swap_pairs(count):
    mates = [(2 * c, 2 * c + 1) for c in range(count // 2)]
    across = [(2 * c + 1, 2 * c + 2) for c in range(count // 2 - 1)]
    both = lambda pairs: pairs + [(b, a) for a, b in pairs]
    return both(mates), both(across)


def dot(a, b, ca, cb):
    return lax.dot_general(a, b, (((ca,), (cb,)), ((), ())), preferred_element_type=F32)


def sigmoid(value):
    return 0.5 * jnp.tanh(0.5 * value) + 0.5


def silu_and_slope(value):
    sig = sigmoid(value)
    lifted = value * sig
    return lifted, sig + lifted - lifted * sig


def call(kernel, outs, scratch, flops, moved, *operands, copied=False):
    floats = pltpu.HBM if copied else pltpu.VMEM
    specs = [
        pl.BlockSpec(memory_space=pltpu.SMEM if o.dtype == jnp.int32 else floats)
        for o in operands
    ]
    single = len(outs) == 1
    shapes = [jax.ShapeDtypeStruct(*o[:2]) for o in outs]
    vmem = [pl.BlockSpec(memory_space=o[2] if len(o) > 2 else pltpu.VMEM) for o in outs]
    return pl.pallas_call(
        kernel,
        out_shape=shapes[0] if single else shapes,
        in_specs=specs,
        out_specs=vmem[0] if single else vmem,
        scratch_shapes=[pltpu.VMEM(*o) if isinstance(o, tuple) else o for o in scratch],
        compiler_params=pltpu.CompilerParams(vmem_limit_bytes=ENCODE_VMEM if copied else 24 << 20),
        cost_estimate=pl.CostEstimate(flops=flops, bytes_accessed=moved, transcendentals=0),
    )(*operands)


def slot_of(block):
    here = lax.axis_index(GRID)
    sign = 1 - 2 * lax.axis_index("core")
    return jnp.clip((block - here) * sign + 1, 0, 2)


def encode_kernel(
    targets, x_hbm, weight_hbm, edges_hbm, across, own, mate, slope_hbm, laid_hbm,
    x, weight, edges, messages, slope, laid, arrived, left,
):
    blocks, picks, rows, cols = edges.shape
    nodes = x.shape[0]
    chunks = 4
    step = nodes // chunks
    pieces = [slice(i * step, (i + 1) * step) for i in range(chunks)]
    weight_in = pltpu.make_async_copy(weight_hbm, weight, arrived.at[0])
    edges_in = pltpu.make_async_copy(edges_hbm, edges, arrived.at[1])
    x_in = [
        pltpu.make_async_copy(x_hbm.at[at], x.at[at], arrived.at[2 + i])
        for i, at in enumerate(pieces)
    ]
    for copy in (weight_in, x_in[0], x_in[1], edges_in, x_in[2], x_in[3]):
        copy.start()
    laid[...] = jnp.zeros_like(laid)

    def encode(i):
        lifted, slanted = silu_and_slope(dot(x[pieces[i], :], weight[...], 1, 0))
        slope[pieces[i], :] = slanted.astype(BF)
        messages[pieces[i], :] = lifted.astype(BF)

    weight_in.wait()
    x_in[0].wait()
    encode(0)
    x_in[1].wait()
    edges_in.wait()
    for b in range(blocks):
        for k in range(picks):
            at = pl.ds(pl.multiple_of(slot_of(targets[k, b]) * rows, rows), rows)
            laid[at, b * cols : (b + 1) * cols] = edges[b, k]
    encode(1)
    laid_out = pltpu.make_async_copy(laid, laid_hbm, left.at[0])
    laid_out.start()
    x_in[2].wait()
    x_in[3].wait()
    encode(2)
    encode(3)
    slope_out = pltpu.make_async_copy(slope, slope_hbm, left.at[1])
    slope_out.start()
    across[...] = dot(laid[:rows, :], messages[...], 1, 0).astype(BF)
    own[...] = dot(laid[rows : 2 * rows, :], messages[...], 1, 0).astype(BF)
    mate[...] = dot(laid[2 * rows :, :], messages[...], 1, 0).astype(BF)
    laid_out.wait()
    slope_out.wait()


def turn_kernel(laid, turned):
    turned[...] = laid[...].T


def sort_kernel(share, x, sorted_x):
    width = x.shape[1]
    row = lax.broadcasted_iota(jnp.int32, (width, width), 0)
    col = lax.broadcasted_iota(jnp.int32, (width, width), 1)
    half = width // 2
    ours = row // half
    inner = row % half
    core = lax.axis_index("core")
    side = jnp.where(ours == 1, core, 1 - core)
    wanted = (inner // share) * (2 * share) + side * share + inner % share
    pick = jnp.where(col == wanted, 1.0, 0.0).astype(BF)
    sorted_x[...] = dot(pick, x[...], 1, 1).astype(BF)


def update_kernel(across, own, mate, latent, weight, updated, again, slope):
    arrived = own[...].astype(F32) + across[...].astype(F32) + mate[...].astype(F32)
    lifted, slanted = silu_and_slope(dot(arrived.astype(BF), weight[...], 1, 0))
    slope[...] = slanted
    fresh = (latent[...].astype(F32) + lifted).astype(BF)
    updated[...] = fresh
    again[...] = fresh


def mix_kernel(sources, mixing, laid, turned):
    rows = mixing.shape[1]
    laid[...] = jnp.zeros_like(laid)
    for k in range(mixing.shape[0]):
        at = pl.ds(pl.multiple_of(slot_of(sources[0, k]) * rows, rows), rows)
        laid[:, at] = mixing[k]
    turned[...] = laid[...].T


def process_kernel(
    across, own, mate, mixing, turned, weight, cotangent, result, to_across, to_own, to_mate, near
):
    rows = own.shape[0]
    near[:rows, :] = across[...]
    near[rows : 2 * rows, :] = own[...]
    near[2 * rows :, :] = mate[...]
    processed = dot(mixing[...], near[...], 1, 0).astype(BF)
    lifted, slanted = silu_and_slope(dot(processed, weight[...], 1, 0))
    result[...] = (own[...].astype(F32) + lifted).astype(BF)
    delta = (cotangent[...].astype(F32) * slanted).astype(BF)
    back = dot(delta, weight[...], 1, 1).astype(BF)
    pushed = dot(turned[...], back, 1, 0).astype(BF)
    to_across[...], to_own[...], to_mate[...] = pushed[:rows], pushed[rows : 2 * rows], pushed[2 * rows :]


def return_kernel(across, own, mate, cotangent, slope, weight, grad, again):
    total = cotangent[...].astype(F32) + own[...].astype(F32)
    total = total + across[...].astype(F32) + mate[...].astype(F32)
    fresh = dot((total * slope[...]).astype(BF), weight[...], 1, 1).astype(BF)
    grad[...] = fresh
    again[...] = fresh


def message_kernel(across, own, mate, turned, slope, sorted_x, delta, theirs, near):
    rows = own.shape[0]
    near[:rows, :] = across[...]
    near[rows : 2 * rows, :] = own[...]
    near[2 * rows :, :] = mate[...]
    nodes = slope.shape[0]
    step = nodes // 4
    for i in range(4):
        at = slice(i * step, (i + 1) * step)
        grad = dot(turned[at, :], near[...], 1, 0)
        delta[at, :] = (grad * slope[at, :].astype(F32)).astype(BF)
    theirs[...] = dot(sorted_x[: theirs.shape[0], :], delta[...], 1, 0).astype(BF)


def gradient_kernel(sorted_x, delta, weight, ours, grid_grad):
    ours[...] = dot(sorted_x[ours.shape[0] :, :], delta[...], 1, 0)
    step = delta.shape[0] // 4
    for i in range(4):
        at = slice(i * step, (i + 1) * step)
        grid_grad[at, :] = dot(delta[at, :], weight[...], 1, 1).astype(BF)


def on_device(
    grid_latent, mesh_latent, cotangent, edge_weights, edge_targets,
    mesh_weights, mesh_sources, encode_weight, aggregate_weight, process_weight,
):
    members = lax.axis_size("ens")
    bands = lax.axis_size(GRID)
    mates, across_pairs = swap_pairs(bands)
    blocks, _, rows, _ = edge_weights.shape
    width = grid_latent.shape[2]
    half = width // 2

    def exchange(to_across, to_mate):
        from_mate = lax.ppermute(to_mate, GRID, mates)
        from_across = lax.ppermute(to_across, GRID, across_pairs)
        return from_across, from_mate

    nodes = blocks * rows
    grid_x = grid_latent[0]
    block = ((rows, width), BF)
    near = ((3 * rows, width), BF)
    to_across, own, to_mate, slope, laid = call(
        encode_kernel,
        [block, block, block, ((nodes, width), BF, pltpu.HBM), ((3 * rows, nodes), BF, pltpu.HBM)],
        [
            (grid_x.shape, BF), (encode_weight.shape, BF), (edge_weights.shape, BF),
            ((nodes, width), BF), ((nodes, width), BF), ((3 * rows, nodes), BF),
            pltpu.SemaphoreType.DMA((6,)), pltpu.SemaphoreType.DMA((2,)),
        ],
        2 * nodes * width * (width + 3 * rows), 4 << 20,
        edge_targets.T, grid_x, encode_weight, edge_weights,
        copied=True,
    )
    across, mate = exchange(to_across, to_mate)
    sources, _ = lax.optimization_barrier((mesh_sources, slope))
    mixing, mixing_turned = call(
        mix_kernel, [((rows, 3 * rows), BF), ((3 * rows, rows), BF)], [], 0, 1 << 18,
        sources, mesh_weights[0],
    )
    own, mixing = lax.optimization_barrier((own, mixing))
    updated, again, mesh_slope = call(
        update_kernel, [block, block, ((rows, width), F32)], [],
        2 * rows * width * width, 1 << 20,
        across, own, mate, mesh_latent[0], aggregate_weight,
    )
    across, mate = exchange(again, updated)
    later, grid_y, _ = lax.optimization_barrier((laid, grid_x, updated))
    turned = call(turn_kernel, [((nodes, 3 * rows), BF)], [], 0, 2 << 20, later)
    result, to_across, own, to_mate = call(
        process_kernel, [block] * 4, [near],
        4 * rows * width * width, 1 << 20,
        across, updated, mate, mixing, mixing_turned, process_weight, cotangent[0],
    )
    across, mate = exchange(to_across, to_mate)
    share = width // bands
    grid_y, _ = lax.optimization_barrier((grid_y, own))
    sorted_x = call(
        functools.partial(sort_kernel, share), [((width, nodes), BF)], [],
        2 * nodes * width * width, 2 << 20,
        grid_y,
    )
    own, sorted_x = lax.optimization_barrier((own, sorted_x))
    agg_grad, again = call(
        return_kernel, [block, block], [],
        2 * rows * width * width, 1 << 20,
        across, own, mate, cotangent[0], mesh_slope, aggregate_weight,
    )
    across, mate = exchange(again, agg_grad)
    enc_delta, theirs = call(
        message_kernel, [((nodes, width), BF), ((half, width), BF)], [near],
        2 * nodes * width * (3 * rows + half), 4 << 20,
        across, agg_grad, mate, turned, slope, sorted_x,
    )
    arrived = lax.ppermute(theirs, GRID, mates)
    ours, grid_grad = call(
        gradient_kernel, [((half, width), F32), ((nodes, width), BF)], [],
        2 * nodes * width * (width + half), 4 << 20,
        sorted_x, enc_delta, encode_weight,
    )
    pair = (ours + arrived.astype(F32)).astype(BF)
    chips = bands // 2
    parts = lax.all_to_all(pair.reshape(chips, share, width), ("y", "z"), 0, 0)
    scale = 1.0 / float(members * nodes * bands) ** 0.5
    summed = parts.astype(F32).sum(0) * scale
    summed = jnp.broadcast_to(summed, (members, share, width))
    final = lax.all_to_all(summed, "ens", 0, 0).sum(0)
    return result[None], grid_grad[None], final


def solution(mesh):
    ens, bands = mesh.devices.shape
    fine = Mesh(mesh.devices.reshape((ens,) + grid_split(bands)), ("ens",) + GRID)
    return jax.shard_map(
        on_device,
        mesh=fine,
        in_specs=(
            P("ens", GRID, None),
            P("ens", GRID, None),
            P("ens", GRID, None),
            P(GRID, None, None, None),
            P(GRID, None),
            P(GRID, None, None, None),
            P(GRID, None),
            P(),
            P(),
            P(),
        ),
        out_specs=(P("ens", GRID, None), P("ens", GRID, None), P(GRID, None)),
        check_vma=False,
    )
```

```python
import functools

import jax
import jax.numpy as jnp
from jax import lax
from jax.experimental import pallas as pl
from jax.experimental.pallas import tpu as pltpu
from jax.sharding import Mesh
from jax.sharding import PartitionSpec as P

BF = jnp.bfloat16
F32 = jnp.float32
ENCODE_VMEM = 55992320
GRID = ("y", "z", "core")


def grid_split(count):
    cores = 2
    chips = count // cores
    ys = 1
    while ys * ys < chips:
        ys *= 2
    return ys, chips // ys, cores


def swap_pairs(count):
    mates = [(2 * c, 2 * c + 1) for c in range(count // 2)]
    across = [(2 * c + 1, 2 * c + 2) for c in range(count // 2 - 1)]
    both = lambda pairs: pairs + [(b, a) for a, b in pairs]
    return both(mates), both(across)


def dot(a, b, ca, cb):
    return lax.dot_general(a, b, (((ca,), (cb,)), ((), ())), preferred_element_type=F32)


def sigmoid(value):
    return 0.5 * jnp.tanh(0.5 * value) + 0.5


def silu_and_slope(value):
    sig = sigmoid(value)
    lifted = value * sig
    return lifted, sig + lifted - lifted * sig


def call(kernel, outs, scratch, flops, moved, *operands, copied=False):
    floats = pltpu.HBM if copied else pltpu.VMEM
    specs = [
        pl.BlockSpec(memory_space=pltpu.SMEM if o.dtype == jnp.int32 else floats)
        for o in operands
    ]
    single = len(outs) == 1
    shapes = [jax.ShapeDtypeStruct(*o[:2]) for o in outs]
    vmem = [pl.BlockSpec(memory_space=o[2] if len(o) > 2 else pltpu.VMEM) for o in outs]
    return pl.pallas_call(
        kernel,
        out_shape=shapes[0] if single else shapes,
        in_specs=specs,
        out_specs=vmem[0] if single else vmem,
        scratch_shapes=[pltpu.VMEM(*o) if isinstance(o, tuple) else o for o in scratch],
        compiler_params=pltpu.CompilerParams(vmem_limit_bytes=ENCODE_VMEM if copied else 24 << 20),
        cost_estimate=pl.CostEstimate(flops=flops, bytes_accessed=moved, transcendentals=0),
    )(*operands)


def slot_of(block):
    here = lax.axis_index(GRID)
    sign = 1 - 2 * lax.axis_index("core")
    return jnp.clip((block - here) * sign + 1, 0, 2)


def encode_kernel(
    targets, x_hbm, weight_hbm, edges_hbm, across, own, mate, laid_hbm,
    x, weight, edges, messages, laid, arrived, left,
):
    blocks, picks, rows, cols = edges.shape
    nodes = x.shape[0]
    chunks = 4
    step = nodes // chunks
    pieces = [slice(i * step, (i + 1) * step) for i in range(chunks)]
    weight_in = pltpu.make_async_copy(weight_hbm, weight, arrived.at[0])
    edges_in = pltpu.make_async_copy(edges_hbm, edges, arrived.at[1])
    x_in = [
        pltpu.make_async_copy(x_hbm.at[at], x.at[at], arrived.at[2 + i])
        for i, at in enumerate(pieces)
    ]
    for copy in (weight_in, x_in[0], x_in[1], edges_in, x_in[2], x_in[3]):
        copy.start()
    laid[...] = jnp.zeros_like(laid)

    def encode(i):
        encoded = dot(x[pieces[i], :], weight[...], 1, 0)
        messages[pieces[i], :] = (encoded * sigmoid(encoded)).astype(BF)

    weight_in.wait()
    x_in[0].wait()
    encode(0)
    x_in[1].wait()
    edges_in.wait()
    for b in range(blocks):
        for k in range(picks):
            at = pl.ds(pl.multiple_of(slot_of(targets[k, b]) * rows, rows), rows)
            laid[at, b * cols : (b + 1) * cols] = edges[b, k]
    encode(1)
    laid_out = pltpu.make_async_copy(laid, laid_hbm, left)
    laid_out.start()
    x_in[2].wait()
    x_in[3].wait()
    encode(2)
    encode(3)
    across[...] = dot(laid[:rows, :], messages[...], 1, 0).astype(BF)
    own[...] = dot(laid[rows : 2 * rows, :], messages[...], 1, 0).astype(BF)
    mate[...] = dot(laid[2 * rows :, :], messages[...], 1, 0).astype(BF)
    laid_out.wait()


def slope_kernel(x, weight, slope):
    step = x.shape[0] // 4
    for i in range(4):
        at = slice(i * step, (i + 1) * step)
        slope[at, :] = silu_and_slope(dot(x[at, :], weight[...], 1, 0))[1].astype(BF)


def turn_kernel(laid, weight, turned, weight_turned):
    turned[...] = laid[...].T
    weight_turned[...] = weight[...].T


def sort_kernel(share, x, sorted_x):
    width = x.shape[1]
    row = lax.broadcasted_iota(jnp.int32, (width, width), 0)
    col = lax.broadcasted_iota(jnp.int32, (width, width), 1)
    half = width // 2
    ours = row // half
    inner = row % half
    core = lax.axis_index("core")
    side = jnp.where(ours == 1, core, 1 - core)
    wanted = (inner // share) * (2 * share) + side * share + inner % share
    pick = jnp.where(col == wanted, 1.0, 0.0).astype(BF)
    sorted_x[...] = dot(pick, x[...], 1, 1).astype(BF)


def update_kernel(across, own, mate, latent, weight, updated, again, slope):
    arrived = own[...].astype(F32) + across[...].astype(F32) + mate[...].astype(F32)
    lifted, slanted = silu_and_slope(dot(arrived.astype(BF), weight[...], 1, 0))
    slope[...] = slanted
    fresh = (latent[...].astype(F32) + lifted).astype(BF)
    updated[...] = fresh
    again[...] = fresh


def mix_kernel(sources, mixing, laid, turned):
    rows = mixing.shape[1]
    laid[...] = jnp.zeros_like(laid)
    for k in range(mixing.shape[0]):
        at = pl.ds(pl.multiple_of(slot_of(sources[0, k]) * rows, rows), rows)
        laid[:, at] = mixing[k]
    turned[...] = laid[...].T


def process_kernel(
    across, own, mate, mixing, turned, weight, cotangent, result, to_across, to_own, to_mate, near
):
    rows = own.shape[0]
    near[:rows, :] = across[...]
    near[rows : 2 * rows, :] = own[...]
    near[2 * rows :, :] = mate[...]
    processed = dot(mixing[...], near[...], 1, 0).astype(BF)
    lifted, slanted = silu_and_slope(dot(processed, weight[...], 1, 0))
    result[...] = (own[...].astype(F32) + lifted).astype(BF)
    delta = (cotangent[...].astype(F32) * slanted).astype(BF)
    back = dot(delta, weight[...], 1, 1).astype(BF)
    pushed = dot(turned[...], back, 1, 0).astype(BF)
    to_across[...], to_own[...], to_mate[...] = pushed[:rows], pushed[rows : 2 * rows], pushed[2 * rows :]


def return_kernel(across, own, mate, cotangent, slope, weight, grad, again):
    total = cotangent[...].astype(F32) + own[...].astype(F32)
    total = total + across[...].astype(F32) + mate[...].astype(F32)
    fresh = dot((total * slope[...]).astype(BF), weight[...], 1, 1).astype(BF)
    grad[...] = fresh
    again[...] = fresh


def message_kernel(across, own, mate, turned, slope, sorted_x, delta, theirs, near):
    rows = own.shape[0]
    near[:rows, :] = across[...]
    near[rows : 2 * rows, :] = own[...]
    near[2 * rows :, :] = mate[...]
    nodes = slope.shape[0]
    step = nodes // 4
    for i in range(4):
        at = slice(i * step, (i + 1) * step)
        grad = dot(turned[at, :], near[...], 1, 0)
        delta[at, :] = (grad * slope[at, :].astype(F32)).astype(BF)
    theirs[...] = dot(sorted_x[: theirs.shape[0], :], delta[...], 1, 0).astype(BF)


def gradient_kernel(sorted_x, delta, weight_turned, ours, grid_grad_hbm, grid_grad, left):
    chunks = 4
    step = delta.shape[0] // chunks
    copies = []
    for i in range(chunks):
        at = slice(i * step, (i + 1) * step)
        grid_grad[at, :] = dot(delta[at, :], weight_turned[...], 1, 0).astype(BF)
        copies.append(pltpu.make_async_copy(grid_grad.at[at], grid_grad_hbm.at[at], left.at[i]))
        copies[i].start()
    ours[...] = dot(sorted_x[ours.shape[0] :, :], delta[...], 1, 0)
    for copy in copies:
        copy.wait()


def on_device(
    grid_latent, mesh_latent, cotangent, edge_weights, edge_targets,
    mesh_weights, mesh_sources, encode_weight, aggregate_weight, process_weight,
):
    members = lax.axis_size("ens")
    bands = lax.axis_size(GRID)
    mates, across_pairs = swap_pairs(bands)
    blocks, _, rows, _ = edge_weights.shape
    width = grid_latent.shape[2]
    half = width // 2

    def exchange(to_across, to_mate):
        from_mate = lax.ppermute(to_mate, GRID, mates)
        from_across = lax.ppermute(to_across, GRID, across_pairs)
        return from_across, from_mate

    nodes = blocks * rows
    grid_x = grid_latent[0]
    block = ((rows, width), BF)
    near = ((3 * rows, width), BF)
    to_across, own, to_mate, laid = call(
        encode_kernel,
        [block, block, block, ((3 * rows, nodes), BF, pltpu.HBM)],
        [
            (grid_x.shape, BF), (encode_weight.shape, BF), (edge_weights.shape, BF),
            ((nodes, width), BF), ((3 * rows, nodes), BF),
            pltpu.SemaphoreType.DMA((6,)), pltpu.SemaphoreType.DMA,
        ],
        2 * nodes * width * (width + 3 * rows), 4 << 20,
        edge_targets.T, grid_x, encode_weight, edge_weights,
        copied=True,
    )
    across, mate = exchange(to_across, to_mate)
    sources, _ = lax.optimization_barrier((mesh_sources, laid))
    mixing, mixing_turned = call(
        mix_kernel, [((rows, 3 * rows), BF), ((3 * rows, rows), BF)], [], 0, 1 << 18,
        sources, mesh_weights[0],
    )
    own, mixing = lax.optimization_barrier((own, mixing))
    updated, again, mesh_slope = call(
        update_kernel, [block, block, ((rows, width), F32)], [],
        2 * rows * width * width, 1 << 20,
        across, own, mate, mesh_latent[0], aggregate_weight,
    )
    across, mate = exchange(again, updated)
    later, grid_y, weight, _ = lax.optimization_barrier((laid, grid_x, encode_weight, updated))
    slope = call(
        slope_kernel, [((nodes, width), BF)], [],
        2 * nodes * width * width, 3 << 20,
        grid_y, weight,
    )
    turned, weight_turned = call(
        turn_kernel, [((nodes, 3 * rows), BF), ((width, width), BF)], [], 0, 2 << 20, later, weight
    )
    updated, slope = lax.optimization_barrier((updated, slope))
    result, to_across, own, to_mate = call(
        process_kernel, [block] * 4, [near],
        4 * rows * width * width, 1 << 20,
        across, updated, mate, mixing, mixing_turned, process_weight, cotangent[0],
    )
    across, mate = exchange(to_across, to_mate)
    share = width // bands
    grid_y, _ = lax.optimization_barrier((grid_y, own))
    sorted_x = call(
        functools.partial(sort_kernel, share), [((width, nodes), BF)], [],
        2 * nodes * width * width, 2 << 20,
        grid_y,
    )
    own, sorted_x = lax.optimization_barrier((own, sorted_x))
    agg_grad, again = call(
        return_kernel, [block, block], [],
        2 * rows * width * width, 1 << 20,
        across, own, mate, cotangent[0], mesh_slope, aggregate_weight,
    )
    across, mate = exchange(again, agg_grad)
    enc_delta, theirs = call(
        message_kernel, [((nodes, width), BF), ((half, width), BF)], [near],
        2 * nodes * width * (3 * rows + half), 4 << 20,
        across, agg_grad, mate, turned, slope, sorted_x,
    )
    arrived = lax.ppermute(theirs, GRID, mates)
    ours, grid_grad = call(
        gradient_kernel,
        [((half, width), F32), ((nodes, width), BF, pltpu.HBM)],
        [((nodes, width), BF), pltpu.SemaphoreType.DMA((4,))],
        2 * nodes * width * (width + half), 4 << 20,
        sorted_x, enc_delta, weight_turned,
    )
    pair = (ours + arrived.astype(F32)).astype(BF)
    chips = bands // 2
    parts = lax.all_to_all(pair.reshape(chips, share, width), ("y", "z"), 0, 0)
    scale = 1.0 / float(members * nodes * bands) ** 0.5
    summed = parts.astype(F32).sum(0) * scale
    summed = jnp.broadcast_to(summed, (members, share, width))
    final = lax.all_to_all(summed, "ens", 0, 0).sum(0)
    return result[None], grid_grad[None], final


def solution(mesh):
    ens, bands = mesh.devices.shape
    fine = Mesh(mesh.devices.reshape((ens,) + grid_split(bands)), ("ens",) + GRID)
    return jax.shard_map(
        on_device,
        mesh=fine,
        in_specs=(
            P("ens", GRID, None),
            P("ens", GRID, None),
            P("ens", GRID, None),
            P(GRID, None, None, None),
            P(GRID, None),
            P(GRID, None, None, None),
            P(GRID, None),
            P(),
            P(),
            P(),
        ),
        out_specs=(P("ens", GRID, None), P("ens", GRID, None), P(GRID, None)),
        check_vma=False,
    )
```

```python
import functools

import jax
import jax.numpy as jnp
from jax import lax
from jax.experimental import pallas as pl
from jax.experimental.pallas import tpu as pltpu
from jax.sharding import Mesh
from jax.sharding import PartitionSpec as P

BF = jnp.bfloat16
F32 = jnp.float32
ENCODE_VMEM = 55992320
GRID = ("y", "z", "core")


def grid_split(count):
    cores = 2
    chips = count // cores
    ys = 1
    while ys * ys < chips:
        ys *= 2
    return ys, chips // ys, cores


def swap_pairs(count):
    mates = [(2 * c, 2 * c + 1) for c in range(count // 2)]
    across = [(2 * c + 1, 2 * c + 2) for c in range(count // 2 - 1)]
    both = lambda pairs: pairs + [(b, a) for a, b in pairs]
    return both(mates), both(across)


def dot(a, b, ca, cb):
    return lax.dot_general(a, b, (((ca,), (cb,)), ((), ())), preferred_element_type=F32)


def sigmoid(value):
    return 0.5 * jnp.tanh(0.5 * value) + 0.5


def silu_and_slope(value):
    sig = sigmoid(value)
    lifted = value * sig
    return lifted, sig + lifted - lifted * sig


def call(kernel, outs, scratch, flops, moved, *operands, copied=False):
    floats = pltpu.HBM if copied else pltpu.VMEM
    specs = [
        pl.BlockSpec(memory_space=pltpu.SMEM if o.dtype == jnp.int32 else floats)
        for o in operands
    ]
    single = len(outs) == 1
    shapes = [jax.ShapeDtypeStruct(*o[:2]) for o in outs]
    vmem = [pl.BlockSpec(memory_space=o[2] if len(o) > 2 else pltpu.VMEM) for o in outs]
    return pl.pallas_call(
        kernel,
        out_shape=shapes[0] if single else shapes,
        in_specs=specs,
        out_specs=vmem[0] if single else vmem,
        scratch_shapes=[pltpu.VMEM(*o) if isinstance(o, tuple) else o for o in scratch],
        compiler_params=pltpu.CompilerParams(vmem_limit_bytes=ENCODE_VMEM if copied else 24 << 20),
        cost_estimate=pl.CostEstimate(flops=flops, bytes_accessed=moved, transcendentals=0),
    )(*operands)


def slot_of(block):
    here = lax.axis_index(GRID)
    sign = 1 - 2 * lax.axis_index("core")
    return jnp.clip((block - here) * sign + 1, 0, 2)


def encode_kernel(
    targets, x_hbm, weight_hbm, edges_hbm, across, own, mate,
    x, weight, edges, messages, laid, arrived,
):
    blocks, picks, rows, cols = edges.shape
    nodes = x.shape[0]
    chunks = 4
    step = nodes // chunks
    pieces = [slice(i * step, (i + 1) * step) for i in range(chunks)]
    weight_in = pltpu.make_async_copy(weight_hbm, weight, arrived.at[0])
    edges_in = pltpu.make_async_copy(edges_hbm, edges, arrived.at[1])
    x_in = [
        pltpu.make_async_copy(x_hbm.at[at], x.at[at], arrived.at[2 + i])
        for i, at in enumerate(pieces)
    ]
    for copy in (weight_in, x_in[0], x_in[1], edges_in, x_in[2], x_in[3]):
        copy.start()
    laid[...] = jnp.zeros_like(laid)

    def encode(i):
        encoded = dot(x[pieces[i], :], weight[...], 1, 0)
        messages[pieces[i], :] = (encoded * sigmoid(encoded)).astype(BF)

    weight_in.wait()
    x_in[0].wait()
    encode(0)
    x_in[1].wait()
    edges_in.wait()
    for b in range(blocks):
        for k in range(picks):
            at = pl.ds(pl.multiple_of(slot_of(targets[k, b]) * rows, rows), rows)
            laid[at, b * cols : (b + 1) * cols] = edges[b, k]
    encode(1)
    x_in[2].wait()
    x_in[3].wait()
    encode(2)
    encode(3)
    across[...] = dot(laid[:rows, :], messages[...], 1, 0).astype(BF)
    own[...] = dot(laid[rows : 2 * rows, :], messages[...], 1, 0).astype(BF)
    mate[...] = dot(laid[2 * rows :, :], messages[...], 1, 0).astype(BF)


def slope_kernel(x, weight, slope):
    step = x.shape[0] // 4
    for i in range(4):
        at = slice(i * step, (i + 1) * step)
        slope[at, :] = silu_and_slope(dot(x[at, :], weight[...], 1, 0))[1].astype(BF)


def turn_kernel(targets, edges, weight, turned, weight_turned):
    blocks, picks, rows, cols = edges.shape
    turned[...] = jnp.zeros_like(turned)
    for b in range(blocks):
        for k in range(picks):
            at = pl.ds(pl.multiple_of(slot_of(targets[k, b]) * rows, rows), rows)
            turned[b * cols : (b + 1) * cols, at] = edges[b, k].T
    weight_turned[...] = weight[...].T


def sort_kernel(share, x, sorted_x):
    width = x.shape[1]
    row = lax.broadcasted_iota(jnp.int32, (width, width), 0)
    col = lax.broadcasted_iota(jnp.int32, (width, width), 1)
    half = width // 2
    ours = row // half
    inner = row % half
    core = lax.axis_index("core")
    side = jnp.where(ours == 1, core, 1 - core)
    wanted = (inner // share) * (2 * share) + side * share + inner % share
    pick = jnp.where(col == wanted, 1.0, 0.0).astype(BF)
    sorted_x[...] = dot(pick, x[...], 1, 1).astype(BF)


def update_kernel(across, own, mate, latent, weight, updated, again, slope):
    arrived = own[...].astype(F32) + across[...].astype(F32) + mate[...].astype(F32)
    lifted, slanted = silu_and_slope(dot(arrived.astype(BF), weight[...], 1, 0))
    slope[...] = slanted
    fresh = (latent[...].astype(F32) + lifted).astype(BF)
    updated[...] = fresh
    again[...] = fresh


def mix_kernel(sources, mixing, laid, turned):
    rows = mixing.shape[1]
    laid[...] = jnp.zeros_like(laid)
    for k in range(mixing.shape[0]):
        at = pl.ds(pl.multiple_of(slot_of(sources[0, k]) * rows, rows), rows)
        laid[:, at] = mixing[k]
    turned[...] = laid[...].T


def process_kernel(
    across, own, mate, mixing, turned, weight, cotangent, result, to_across, to_own, to_mate, near
):
    rows = own.shape[0]
    near[:rows, :] = across[...]
    near[rows : 2 * rows, :] = own[...]
    near[2 * rows :, :] = mate[...]
    processed = dot(mixing[...], near[...], 1, 0).astype(BF)
    lifted, slanted = silu_and_slope(dot(processed, weight[...], 1, 0))
    result[...] = (own[...].astype(F32) + lifted).astype(BF)
    delta = (cotangent[...].astype(F32) * slanted).astype(BF)
    back = dot(delta, weight[...], 1, 1).astype(BF)
    pushed = dot(turned[...], back, 1, 0).astype(BF)
    to_across[...], to_own[...], to_mate[...] = pushed[:rows], pushed[rows : 2 * rows], pushed[2 * rows :]


def return_kernel(across, own, mate, cotangent, slope, weight, grad, again):
    total = cotangent[...].astype(F32) + own[...].astype(F32)
    total = total + across[...].astype(F32) + mate[...].astype(F32)
    fresh = dot((total * slope[...]).astype(BF), weight[...], 1, 1).astype(BF)
    grad[...] = fresh
    again[...] = fresh


def message_kernel(across, own, mate, turned, slope, sorted_x, delta, theirs, near):
    rows = own.shape[0]
    near[:rows, :] = across[...]
    near[rows : 2 * rows, :] = own[...]
    near[2 * rows :, :] = mate[...]
    nodes = slope.shape[0]
    step = nodes // 4
    for i in range(4):
        at = slice(i * step, (i + 1) * step)
        grad = dot(turned[at, :], near[...], 1, 0)
        delta[at, :] = (grad * slope[at, :].astype(F32)).astype(BF)
    theirs[...] = dot(sorted_x[: theirs.shape[0], :], delta[...], 1, 0).astype(BF)


def gradient_kernel(sorted_x, delta, weight_turned, ours, grid_grad_hbm, grid_grad, left):
    chunks = 4
    step = delta.shape[0] // chunks
    copies = []
    for i in range(chunks):
        at = slice(i * step, (i + 1) * step)
        grid_grad[at, :] = dot(delta[at, :], weight_turned[...], 1, 0).astype(BF)
        copies.append(pltpu.make_async_copy(grid_grad.at[at], grid_grad_hbm.at[at], left.at[i]))
        copies[i].start()
    ours[...] = dot(sorted_x[ours.shape[0] :, :], delta[...], 1, 0)
    for copy in copies:
        copy.wait()


def on_device(
    grid_latent, mesh_latent, cotangent, edge_weights, edge_targets,
    mesh_weights, mesh_sources, encode_weight, aggregate_weight, process_weight,
):
    members = lax.axis_size("ens")
    bands = lax.axis_size(GRID)
    mates, across_pairs = swap_pairs(bands)
    blocks, _, rows, _ = edge_weights.shape
    width = grid_latent.shape[2]
    half = width // 2

    def exchange(to_across, to_mate):
        from_mate = lax.ppermute(to_mate, GRID, mates)
        from_across = lax.ppermute(to_across, GRID, across_pairs)
        return from_across, from_mate

    nodes = blocks * rows
    grid_x = grid_latent[0]
    block = ((rows, width), BF)
    near = ((3 * rows, width), BF)
    to_across, own, to_mate = call(
        encode_kernel,
        [block, block, block],
        [
            (grid_x.shape, BF), (encode_weight.shape, BF), (edge_weights.shape, BF),
            ((nodes, width), BF), ((3 * rows, nodes), BF),
            pltpu.SemaphoreType.DMA((6,)),
        ],
        2 * nodes * width * (width + 3 * rows), 4 << 20,
        edge_targets.T, grid_x, encode_weight, edge_weights,
        copied=True,
    )
    across, mate = exchange(to_across, to_mate)
    sources, _ = lax.optimization_barrier((mesh_sources, own))
    mixing, mixing_turned = call(
        mix_kernel, [((rows, 3 * rows), BF), ((3 * rows, rows), BF)], [], 0, 1 << 18,
        sources, mesh_weights[0],
    )
    own, mixing = lax.optimization_barrier((own, mixing))
    updated, again, mesh_slope = call(
        update_kernel, [block, block, ((rows, width), F32)], [],
        2 * rows * width * width, 1 << 20,
        across, own, mate, mesh_latent[0], aggregate_weight,
    )
    across, mate = exchange(again, updated)
    targets, edges, grid_y, weight, _ = lax.optimization_barrier(
        (edge_targets.T, edge_weights, grid_x, encode_weight, updated)
    )
    slope = call(
        slope_kernel, [((nodes, width), BF)], [],
        2 * nodes * width * width, 3 << 20,
        grid_y, weight,
    )
    turned, weight_turned = call(
        turn_kernel, [((nodes, 3 * rows), BF), ((width, width), BF)], [], 0, 2 << 20,
        targets, edges, weight,
    )
    updated, slope = lax.optimization_barrier((updated, slope))
    result, to_across, own, to_mate = call(
        process_kernel, [block] * 4, [near],
        4 * rows * width * width, 1 << 20,
        across, updated, mate, mixing, mixing_turned, process_weight, cotangent[0],
    )
    across, mate = exchange(to_across, to_mate)
    share = width // bands
    grid_y, _ = lax.optimization_barrier((grid_y, own))
    sorted_x = call(
        functools.partial(sort_kernel, share), [((width, nodes), BF)], [],
        2 * nodes * width * width, 2 << 20,
        grid_y,
    )
    own, sorted_x = lax.optimization_barrier((own, sorted_x))
    agg_grad, again = call(
        return_kernel, [block, block], [],
        2 * rows * width * width, 1 << 20,
        across, own, mate, cotangent[0], mesh_slope, aggregate_weight,
    )
    across, mate = exchange(again, agg_grad)
    enc_delta, theirs = call(
        message_kernel, [((nodes, width), BF), ((half, width), BF)], [near],
        2 * nodes * width * (3 * rows + half), 4 << 20,
        across, agg_grad, mate, turned, slope, sorted_x,
    )
    arrived = lax.ppermute(theirs, GRID, mates)
    ours, grid_grad = call(
        gradient_kernel,
        [((half, width), F32), ((nodes, width), BF, pltpu.HBM)],
        [((nodes, width), BF), pltpu.SemaphoreType.DMA((4,))],
        2 * nodes * width * (width + half), 4 << 20,
        sorted_x, enc_delta, weight_turned,
    )
    pair = (ours + arrived.astype(F32)).astype(BF)
    chips = bands // 2
    parts = lax.all_to_all(pair.reshape(chips, share, width), ("y", "z"), 0, 0)
    scale = 1.0 / float(members * nodes * bands) ** 0.5
    summed = parts.astype(F32).sum(0) * scale
    summed = jnp.broadcast_to(summed, (members, share, width))
    final = lax.all_to_all(summed, "ens", 0, 0).sum(0)
    return result[None], grid_grad[None], final


def solution(mesh):
    ens, bands = mesh.devices.shape
    fine = Mesh(mesh.devices.reshape((ens,) + grid_split(bands)), ("ens",) + GRID)
    return jax.shard_map(
        on_device,
        mesh=fine,
        in_specs=(
            P("ens", GRID, None),
            P("ens", GRID, None),
            P("ens", GRID, None),
            P(GRID, None, None, None),
            P(GRID, None),
            P(GRID, None, None, None),
            P(GRID, None),
            P(),
            P(),
            P(),
        ),
        out_specs=(P("ens", GRID, None), P("ens", GRID, None), P(GRID, None)),
        check_vma=False,
    )
```

```python
import functools

import jax
import jax.numpy as jnp
from jax import lax
from jax.experimental import pallas as pl
from jax.experimental.pallas import tpu as pltpu
from jax.sharding import Mesh
from jax.sharding import PartitionSpec as P

BF = jnp.bfloat16
F32 = jnp.float32
ENCODE_VMEM = 55992320
GRID = ("y", "z", "core")


def grid_split(count):
    cores = 2
    chips = count // cores
    ys = 1
    while ys * ys < chips:
        ys *= 2
    return ys, chips // ys, cores


def swap_pairs(count):
    mates = [(2 * c, 2 * c + 1) for c in range(count // 2)]
    across = [(2 * c + 1, 2 * c + 2) for c in range(count // 2 - 1)]
    both = lambda pairs: pairs + [(b, a) for a, b in pairs]
    return both(mates), both(across)


def dot(a, b, ca, cb):
    return lax.dot_general(a, b, (((ca,), (cb,)), ((), ())), preferred_element_type=F32)


def sigmoid(value):
    return 0.5 * jnp.tanh(0.5 * value) + 0.5


def silu_and_slope(value):
    sig = sigmoid(value)
    lifted = value * sig
    return lifted, sig + lifted - lifted * sig


def call(kernel, outs, scratch, flops, moved, *operands, copied=False):
    floats = pltpu.HBM if copied else pltpu.VMEM
    specs = [
        pl.BlockSpec(memory_space=pltpu.SMEM if o.dtype == jnp.int32 else floats)
        for o in operands
    ]
    single = len(outs) == 1
    shapes = [jax.ShapeDtypeStruct(*o[:2]) for o in outs]
    vmem = [pl.BlockSpec(memory_space=o[2] if len(o) > 2 else pltpu.VMEM) for o in outs]
    return pl.pallas_call(
        kernel,
        out_shape=shapes[0] if single else shapes,
        in_specs=specs,
        out_specs=vmem[0] if single else vmem,
        scratch_shapes=[pltpu.VMEM(*o) if isinstance(o, tuple) else o for o in scratch],
        compiler_params=pltpu.CompilerParams(vmem_limit_bytes=ENCODE_VMEM if copied else 24 << 20),
        cost_estimate=pl.CostEstimate(flops=flops, bytes_accessed=moved, transcendentals=0),
    )(*operands)


def slot_of(block):
    here = lax.axis_index(GRID)
    sign = 1 - 2 * lax.axis_index("core")
    return jnp.clip((block - here) * sign + 1, 0, 2)


def encode_kernel(
    targets, x_hbm, weight_hbm, edges_hbm, across, own, mate,
    x, weight, edges, messages, laid, arrived,
):
    blocks, picks, rows, cols = edges.shape
    nodes = x.shape[0]
    chunks = 4
    step = nodes // chunks
    pieces = [slice(i * step, (i + 1) * step) for i in range(chunks)]
    weight_in = pltpu.make_async_copy(weight_hbm, weight, arrived.at[0])
    edges_in = pltpu.make_async_copy(edges_hbm, edges, arrived.at[1])
    x_in = [
        pltpu.make_async_copy(x_hbm.at[at], x.at[at], arrived.at[2 + i])
        for i, at in enumerate(pieces)
    ]
    for copy in (weight_in, x_in[0], x_in[1], edges_in, x_in[2], x_in[3]):
        copy.start()
    laid[...] = jnp.zeros_like(laid)

    def encode(i):
        encoded = dot(x[pieces[i], :], weight[...], 1, 0)
        messages[pieces[i], :] = (encoded * sigmoid(encoded)).astype(BF)

    weight_in.wait()
    x_in[0].wait()
    encode(0)
    x_in[1].wait()
    edges_in.wait()
    for b in range(blocks):
        for k in range(picks):
            at = pl.ds(pl.multiple_of(slot_of(targets[k, b]) * rows, rows), rows)
            laid[at, b * cols : (b + 1) * cols] = edges[b, k]
    encode(1)
    x_in[2].wait()
    x_in[3].wait()
    encode(2)
    encode(3)
    across[...] = dot(laid[:rows, :], messages[...], 1, 0).astype(BF)
    own[...] = dot(laid[rows : 2 * rows, :], messages[...], 1, 0).astype(BF)
    mate[...] = dot(laid[2 * rows :, :], messages[...], 1, 0).astype(BF)


def slope_kernel(x, weight, slope):
    step = x.shape[0] // 4
    for i in range(4):
        at = slice(i * step, (i + 1) * step)
        slope[at, :] = silu_and_slope(dot(x[at, :], weight[...], 1, 0))[1].astype(BF)


def turn_kernel(targets, edges, weight, turned, weight_turned):
    blocks, picks, rows, cols = edges.shape
    turned[...] = jnp.zeros_like(turned)
    for b in range(blocks):
        for k in range(picks):
            at = pl.ds(pl.multiple_of(slot_of(targets[k, b]) * rows, rows), rows)
            turned[b * cols : (b + 1) * cols, at] = edges[b, k].T
    weight_turned[...] = weight[...].T


def sort_kernel(share, x, sorted_x):
    width = x.shape[1]
    row = lax.broadcasted_iota(jnp.int32, (width, width), 0)
    col = lax.broadcasted_iota(jnp.int32, (width, width), 1)
    half = width // 2
    ours = row // half
    inner = row % half
    core = lax.axis_index("core")
    side = jnp.where(ours == 1, core, 1 - core)
    wanted = (inner // share) * (2 * share) + side * share + inner % share
    pick = jnp.where(col == wanted, 1.0, 0.0).astype(BF)
    sorted_x[...] = dot(pick, x[...], 1, 1).astype(BF)


def update_kernel(across, own, mate, latent, weight, updated, again, slope):
    arrived = own[...].astype(F32) + across[...].astype(F32) + mate[...].astype(F32)
    lifted, slanted = silu_and_slope(dot(arrived.astype(BF), weight[...], 1, 0))
    slope[...] = slanted
    fresh = (latent[...].astype(F32) + lifted).astype(BF)
    updated[...] = fresh
    again[...] = fresh


def mix_kernel(sources, mixing, weight, laid, turned, weight_turned):
    rows = mixing.shape[1]
    laid[...] = jnp.zeros_like(laid)
    for k in range(mixing.shape[0]):
        at = pl.ds(pl.multiple_of(slot_of(sources[0, k]) * rows, rows), rows)
        laid[:, at] = mixing[k]
    turned[...] = laid[...].T
    weight_turned[...] = weight[...].T


def process_kernel(
    across, own, mate, mixing, turned, weight, cotangent, result, to_across, to_own, to_mate, near
):
    rows = own.shape[0]
    near[:rows, :] = across[...]
    near[rows : 2 * rows, :] = own[...]
    near[2 * rows :, :] = mate[...]
    processed = dot(mixing[...], near[...], 1, 0).astype(BF)
    lifted, slanted = silu_and_slope(dot(processed, weight[...], 1, 0))
    result[...] = (own[...].astype(F32) + lifted).astype(BF)
    delta = (cotangent[...].astype(F32) * slanted).astype(BF)
    back = dot(delta, weight[...], 1, 1).astype(BF)
    pushed = dot(turned[...], back, 1, 0).astype(BF)
    to_across[...], to_own[...], to_mate[...] = pushed[:rows], pushed[rows : 2 * rows], pushed[2 * rows :]


def return_kernel(across, own, mate, cotangent, slope, weight_turned, grad, again):
    total = cotangent[...].astype(F32) + own[...].astype(F32)
    total = total + across[...].astype(F32) + mate[...].astype(F32)
    fresh = dot((total * slope[...]).astype(BF), weight_turned[...], 1, 0).astype(BF)
    grad[...] = fresh
    again[...] = fresh


def message_kernel(across, own, mate, turned, slope, sorted_x, delta, theirs, near):
    rows = own.shape[0]
    near[:rows, :] = across[...]
    near[rows : 2 * rows, :] = own[...]
    near[2 * rows :, :] = mate[...]
    nodes = slope.shape[0]
    step = nodes // 4
    for i in range(4):
        at = slice(i * step, (i + 1) * step)
        grad = dot(turned[at, :], near[...], 1, 0)
        delta[at, :] = (grad * slope[at, :].astype(F32)).astype(BF)
    theirs[...] = dot(sorted_x[: theirs.shape[0], :], delta[...], 1, 0).astype(BF)


def gradient_kernel(sorted_x, delta, weight_turned, ours, grid_grad_hbm, grid_grad, left):
    chunks = 4
    step = delta.shape[0] // chunks
    copies = []
    for i in range(chunks):
        at = slice(i * step, (i + 1) * step)
        grid_grad[at, :] = dot(delta[at, :], weight_turned[...], 1, 0).astype(BF)
        copies.append(pltpu.make_async_copy(grid_grad.at[at], grid_grad_hbm.at[at], left.at[i]))
        copies[i].start()
    ours[...] = dot(sorted_x[ours.shape[0] :, :], delta[...], 1, 0)
    for copy in copies:
        copy.wait()


def on_device(
    grid_latent, mesh_latent, cotangent, edge_weights, edge_targets,
    mesh_weights, mesh_sources, encode_weight, aggregate_weight, process_weight,
):
    members = lax.axis_size("ens")
    bands = lax.axis_size(GRID)
    mates, across_pairs = swap_pairs(bands)
    blocks, _, rows, _ = edge_weights.shape
    width = grid_latent.shape[2]
    half = width // 2

    def exchange(to_across, to_mate):
        from_mate = lax.ppermute(to_mate, GRID, mates)
        from_across = lax.ppermute(to_across, GRID, across_pairs)
        return from_across, from_mate

    nodes = blocks * rows
    grid_x = grid_latent[0]
    block = ((rows, width), BF)
    near = ((3 * rows, width), BF)
    to_across, own, to_mate = call(
        encode_kernel,
        [block, block, block],
        [
            (grid_x.shape, BF), (encode_weight.shape, BF), (edge_weights.shape, BF),
            ((nodes, width), BF), ((3 * rows, nodes), BF),
            pltpu.SemaphoreType.DMA((6,)),
        ],
        2 * nodes * width * (width + 3 * rows), 4 << 20,
        edge_targets.T, grid_x, encode_weight, edge_weights,
        copied=True,
    )
    across, mate = exchange(to_across, to_mate)
    sources, _ = lax.optimization_barrier((mesh_sources, own))
    mixing, mixing_turned, aggregate_turned = call(
        mix_kernel, [((rows, 3 * rows), BF), ((3 * rows, rows), BF), ((width, width), BF)], [],
        0, 1 << 20,
        sources, mesh_weights[0], aggregate_weight,
    )
    own, mixing = lax.optimization_barrier((own, mixing))
    updated, again, mesh_slope = call(
        update_kernel, [block, block, ((rows, width), F32)], [],
        2 * rows * width * width, 1 << 20,
        across, own, mate, mesh_latent[0], aggregate_weight,
    )
    across, mate = exchange(again, updated)
    targets, edges, grid_y, weight, _ = lax.optimization_barrier(
        (edge_targets.T, edge_weights, grid_x, encode_weight, updated)
    )
    slope = call(
        slope_kernel, [((nodes, width), BF)], [],
        2 * nodes * width * width, 3 << 20,
        grid_y, weight,
    )
    turned, weight_turned = call(
        turn_kernel, [((nodes, 3 * rows), BF), ((width, width), BF)], [], 0, 2 << 20,
        targets, edges, weight,
    )
    updated, slope = lax.optimization_barrier((updated, slope))
    result, to_across, own, to_mate = call(
        process_kernel, [block] * 4, [near],
        4 * rows * width * width, 1 << 20,
        across, updated, mate, mixing, mixing_turned, process_weight, cotangent[0],
    )
    across, mate = exchange(to_across, to_mate)
    share = width // bands
    grid_y, _ = lax.optimization_barrier((grid_y, own))
    sorted_x = call(
        functools.partial(sort_kernel, share), [((width, nodes), BF)], [],
        2 * nodes * width * width, 2 << 20,
        grid_y,
    )
    own, sorted_x = lax.optimization_barrier((own, sorted_x))
    agg_grad, again = call(
        return_kernel, [block, block], [],
        2 * rows * width * width, 1 << 20,
        across, own, mate, cotangent[0], mesh_slope, aggregate_turned,
    )
    across, mate = exchange(again, agg_grad)
    enc_delta, theirs = call(
        message_kernel, [((nodes, width), BF), ((half, width), BF)], [near],
        2 * nodes * width * (3 * rows + half), 4 << 20,
        across, agg_grad, mate, turned, slope, sorted_x,
    )
    arrived = lax.ppermute(theirs, GRID, mates)
    ours, grid_grad = call(
        gradient_kernel,
        [((half, width), F32), ((nodes, width), BF, pltpu.HBM)],
        [((nodes, width), BF), pltpu.SemaphoreType.DMA((4,))],
        2 * nodes * width * (width + half), 4 << 20,
        sorted_x, enc_delta, weight_turned,
    )
    pair = (ours + arrived.astype(F32)).astype(BF)
    chips = bands // 2
    parts = lax.all_to_all(pair.reshape(chips, share, width), ("y", "z"), 0, 0)
    scale = 1.0 / float(members * nodes * bands) ** 0.5
    summed = parts.astype(F32).sum(0) * scale
    summed = jnp.broadcast_to(summed, (members, share, width))
    final = lax.all_to_all(summed, "ens", 0, 0).sum(0)
    return result[None], grid_grad[None], final


def solution(mesh):
    ens, bands = mesh.devices.shape
    fine = Mesh(mesh.devices.reshape((ens,) + grid_split(bands)), ("ens",) + GRID)
    return jax.shard_map(
        on_device,
        mesh=fine,
        in_specs=(
            P("ens", GRID, None),
            P("ens", GRID, None),
            P("ens", GRID, None),
            P(GRID, None, None, None),
            P(GRID, None),
            P(GRID, None, None, None),
            P(GRID, None),
            P(),
            P(),
            P(),
        ),
        out_specs=(P("ens", GRID, None), P("ens", GRID, None), P(GRID, None)),
        check_vma=False,
    )
```
